32 devices in a mesh: parts: 2 (over y), shard: 4 (over z), ckpt: 2 (over x), sub: 2 (over core).
Axes of the slice: x: 2, y: 2, z: 4, core: 2. Of those that a mesh axis runs over, the one named last changes fastest.
Arguments:
- train_grads: bfloat16 [2, 6144, 16384], P('ckpt', ('parts', 'shard'), 'sub'), parts along dimension 1, may hold values from -0.046875 to 0.046875
- query_grads: float32 [2, 256, 16384], P('ckpt', ('parts', 'shard'), 'sub'), parts along dimension 1, may hold values from -6 to 6
- precond: float32 [2, 16384], P('ckpt', 'sub'), may hold values from 0.3 to 3
- learn_rates: float32 [64], replicated, may hold values from 0.25 to 2.5
- ckpt_order: int32 [2], replicated, may hold values from 0 to 63
Outputs:
- scores: float32 [128, 6144], P(('ckpt', 'sub'), ('parts', 'shard')), parts along dimension 1
The draws below stay inside these ranges and needn't reach their ends.
There are 2 independent parts, one for each index of `parts`. The reference program is written for one: setup_inputs(seed, part) draws one part's arguments, and reference() takes and returns one part's arrays. A program takes and returns all parts, laid end to end along the dimension named above; an argument that names none is the same for every part. Nothing has to cross between parts.
All inputs are finite; a program needn't handle non-finite values.
Results may differ from the reference program's by a relative error of at most 0.0029.
Values may be sent and summed in bfloat16 or wider, within the bound.
No kernel may reach another device: no remote copies, remote signals or barrier semaphores. Data moves between devices by JAX's collectives and lax.ppermute only.
A program may use at most 128 MiB of HBM per device.

```python
import math
import jax
import jax.numpy as jnp

K = 16384
LR_STEPS = 64
TRAIN = 3072
QUERIES = 128
CKPTS = 2


def shard_levels(own_key, extent, split, least, top_value):
    factor_of = 1.0
    for dim, shards_of in split:
        draws = jax.random.uniform(jax.random.fold_in(jax.random.fold_in(own_key, 6), dim), (shards_of,), jnp.float32, least / len(split), top_value / len(split))
        factor_of = factor_of * jnp.repeat(jnp.exp(draws), extent[dim] // shards_of).reshape((-1,) + (1,) * (len(extent) - 1 - dim))
    return factor_of


def normal_values(rng, dims, deviation, limit, shards=(), dtype=jnp.bfloat16):
    result = deviation * jax.random.normal(rng, dims, jnp.float32)
    if shards:
        result = result * shard_levels(rng, dims, shards, -0.22, 0.18)
    return jnp.clip(result, -limit, limit).astype(dtype)


def setup_inputs(seed: int = 0, part: int = 0) -> dict:
    keys = jax.random.split(jax.random.key(seed), 6)
    part_keys = jax.random.split(jax.random.fold_in(keys[5], part), 6)
    train_grads = normal_values(part_keys[0], (CKPTS, TRAIN, K), K ** -0.5, 0.046875, ((0, 2), (1, 4), (2, 2)))
    query_grads = normal_values(part_keys[1], (CKPTS, QUERIES, K), 1.0, 6.0, ((0, 2), (1, 4), (2, 2)), jnp.float32)
    precond = jnp.clip(jnp.exp(math.log(3.0) - 2.3025851 * jax.random.uniform(keys[2], (CKPTS, K), jnp.float32) ** shard_levels(keys[2], (CKPTS, K), ((0, 2), (1, 2)), -0.2, 0.2)), 0.3, 3.0)
    learn_rates = jnp.clip(jnp.exp(jax.random.uniform(keys[3], (LR_STEPS,), jnp.float32, math.log(0.25), math.log(2.5))), 0.25, 2.5)
    ckpt_order = jax.random.randint(keys[4], (CKPTS,), 0, LR_STEPS).astype(jnp.int32)
    return dict(train_grads=train_grads, query_grads=query_grads, precond=precond, learn_rates=learn_rates, ckpt_order=ckpt_order)


def reference(train_grads, query_grads, precond, learn_rates, ckpt_order):
    total = jnp.zeros((QUERIES, TRAIN), jnp.float32)
    step_rates = learn_rates[ckpt_order.astype(jnp.int32)]
    for index in range(CKPTS):
        conditioned = (query_grads[index] * precond[index][None, :]).astype(jnp.bfloat16)
        partial_value = jnp.dot(conditioned, train_grads[index].T, preferred_element_type=jnp.float32)
        total = total + step_rates[index] * partial_value
    return total
```

```python
import jax
import jax.numpy as jnp
from jax import lax
from jax.sharding import PartitionSpec as P

CHUNKS = 4
AXES = ("parts", "shard", "ckpt", "sub")


def line_ring(n):
    odd = list(range(1, n, 2))
    even = list(range(0, n, 2))
    return [0] + odd + even[:0:-1]


def ring_position(z, n):
    return jnp.where(z == 0, 0, jnp.where(z % 2 == 1, (z + 1) // 2, n - z // 2))


def score_rows(block_rows, train_rows):
    return lax.dot_general(
        block_rows, train_rows, (((1,), (1,)), ((), ())), preferred_element_type=jnp.float32
    )


def per_device(sizes, train_grads, query_grads, precond, learn_rates, ckpt_order):
    train_local = train_grads[0]
    query_local = query_grads[0]
    parts, shards, ckpts, subs = sizes
    groups = ckpts * subs
    ring = line_ring(shards)
    place = {z: i for i, z in enumerate(ring)}
    hops = [(ring[i], ring[(i + 1) % shards]) for i in range(shards)] if shards > 1 else []
    per_group = shards // groups

    width = query_local.shape[1] // CHUNKS
    current = [
        (query_local[:, j * width : (j + 1) * width] * precond[:, j * width : (j + 1) * width]).astype(jnp.bfloat16)
        for j in range(CHUNKS)
    ]

    holder = lax.axis_index("ckpt")
    positions = jnp.arange(ckpt_order.shape[0], dtype=jnp.int32)
    number = jnp.sum(jnp.where(positions == holder, ckpt_order, 0))
    table_steps = jnp.arange(learn_rates.shape[0], dtype=jnp.int32)
    step_rate = jnp.sum(jnp.where(table_steps == number, learn_rates, 0.0))

    sums = []
    for step in range(shards):
        total = None
        following = []
        for j in range(CHUNKS):
            if step < shards - 1:
                following.append(lax.ppermute(current[j], "shard", hops))
            piece = score_rows(current[j], train_local[:, j * width : (j + 1) * width])
            total = piece if total is None else total + piece
        sums.append(total)
        current = following

    me = lax.axis_index("shard")
    my_place = ring_position(me, shards)
    my_group = lax.axis_index(("ckpt", "sub"))

    def blocks_of(group):
        rows = []
        for k in range(per_group):
            step = (my_place - ring_position(group * per_group + k, shards)) % shards
            value = jnp.zeros_like(sums[0])
            for s in range(shards - 1):
                value = jnp.where(step == s, sums[s], value)
            rows.append(value)
        return jnp.concatenate(rows, axis=0) * step_rate

    def last_of(z):
        return ring[(place[z] + 1) % shards]

    def device(p, z, g):
        return ((p * shards + z) * ckpts + g // subs) * subs + g % subs

    result = blocks_of(my_group)
    for d in range(1, groups):
        pairs = [
            (device(p, z, g), device(p, z, (g + d) % groups))
            for p in range(parts)
            for z in range(shards)
            for g in range(groups)
            if per_group > 1 or last_of(z) != (g + d) % groups
        ]
        result = result + lax.ppermute(blocks_of((my_group + d) % groups), AXES, pairs)

    last = sums[-1] * step_rate
    late = jnp.where((last_of_traced(my_place, shards) // per_group) == my_group, last, 0.0)
    for d in range(1, groups):
        pairs = [
            (device(p, z, g), device(p, z, (g + d) % groups))
            for p in range(parts)
            for z in range(shards)
            for g in range(groups)
            if last_of(z) // per_group == (g + d) % groups
        ]
        late = late + lax.ppermute(last, AXES, pairs)
    if per_group == 1:
        return result + late
    slot = last_of_traced(my_place, shards) % per_group
    rows = late.shape[0]
    return lax.dynamic_update_slice_in_dim(
        result, lax.dynamic_slice_in_dim(result, slot * rows, rows, 0) + late, slot * rows, 0
    )


def last_of_traced(my_place, n):
    p = (my_place + 1) % n
    return jnp.where(p <= n // 2, jnp.maximum(2 * p - 1, 0), 2 * (n - p))


def solution(mesh):
    sizes = tuple(mesh.shape[a] for a in AXES)

    def run(*args):
        return per_device(sizes, *args)

    return jax.shard_map(
        run,
        mesh=mesh,
        in_specs=(
            P("ckpt", ("parts", "shard"), "sub"),
            P("ckpt", ("parts", "shard"), "sub"),
            P("ckpt", "sub"),
            P(),
            P(),
        ),
        out_specs=P(("ckpt", "sub"), ("parts", "shard")),
        check_vma=False,
    )
```

```python
import jax
import jax.numpy as jnp
from jax import lax
from jax.experimental import pallas as pl
from jax.experimental.pallas import tpu as pltpu
from jax.sharding import PartitionSpec as P

CHUNKS = (6, 6, 4)
AXES = ("parts", "shard", "ckpt", "sub")
VMEM = pl.BlockSpec(memory_space=pltpu.VMEM)
SMEM = pl.BlockSpec(memory_space=pltpu.SMEM)
HBM = pl.BlockSpec(memory_space=pltpu.HBM)
ANY = pl.BlockSpec(memory_space=pl.ANY)
PIECES = 4


def line_ring(n):
    odd = list(range(1, n, 2))
    even = list(range(0, n, 2))
    return [0] + odd + even[:0:-1]


def ring_position(z, n):
    return jnp.where(z == 0, 0, jnp.where(z % 2 == 1, (z + 1) // 2, n - z // 2))


def chip_at(p, n):
    return jnp.where(p <= n // 2, jnp.maximum(2 * p - 1, 0), 2 * (n - p))


def call(kernel, name, shapes, specs, args, limit=8, scratch=(), flops=0, aliases=None):
    return pl.pallas_call(
        kernel,
        in_specs=specs,
        out_specs=[VMEM] * len(shapes),
        out_shape=shapes,
        scratch_shapes=scratch,
        input_output_aliases=aliases or {},
        compiler_params=pltpu.CompilerParams(vmem_limit_bytes=limit << 20),
        cost_estimate=pl.CostEstimate(flops=flops, bytes_accessed=0, transcendentals=0),
        name=name,
    )(*args)


def times(rows, train_part):
    return lax.dot_general(
        rows, train_part, (((1,), (1,)), ((), ())), preferred_element_type=jnp.float32
    )


def condition(query, precond, spans):
    rows = query.shape[0]
    count = len(spans)
    first, total = spans[0][0], sum(width for _, width in spans)

    def kernel(query_ref, precond_ref, *refs):
        outs, (held, scale, sems) = refs[:count], refs[count:]
        copies = [pltpu.make_async_copy(precond_ref.at[:, pl.ds(first, total)], scale, sems.at[count])]
        copies += [
            pltpu.make_async_copy(
                query_ref.at[:, pl.ds(start, width)], held.at[:, pl.ds(start - first, width)], sems.at[i]
            )
            for i, (start, width) in enumerate(spans)
        ]
        for copy in copies:
            copy.start()
        copies[0].wait()
        for i, (start, width) in enumerate(spans):
            copies[i + 1].wait()
            at = pl.ds(start - first, width)
            outs[i][...] = (held[:, at] * scale[:, at]).astype(jnp.bfloat16)

    return call(
        kernel,
        "condition",
        [jax.ShapeDtypeStruct((rows, width), jnp.bfloat16) for _, width in spans],
        [HBM, HBM],
        (query, precond),
        scratch=[
            pltpu.VMEM((rows, total), jnp.float32),
            pltpu.VMEM((1, total), jnp.float32),
            pltpu.SemaphoreType.DMA((count + 1,)),
        ],
    )


def fetch(train, span):
    start, width = span
    count = train.shape[0]
    tall = count // PIECES

    def kernel(train_ref, held, sems):
        copies = [
            pltpu.make_async_copy(
                train_ref.at[pl.ds(i * tall, tall), pl.ds(start, width)], held.at[pl.ds(i * tall, tall), :], sems.at[i]
            )
            for i in range(PIECES)
        ]
        for copy in copies:
            copy.start()
        for copy in copies:
            copy.wait()

    return call(
        kernel,
        "fetch",
        [pltpu.VMEM((count, width), train.dtype)],
        [ANY],
        (train,),
        scratch=[pltpu.SemaphoreType.DMA((PIECES,))],
        flops=2 * 512 * width * count,
    )[0]


def rate_row(learn_rates, ckpt_order, columns):
    def kernel(rates_ref, order_ref, row, rates, order, sems):
        copies = [
            pltpu.make_async_copy(rates_ref, rates, sems.at[0]),
            pltpu.make_async_copy(order_ref, order, sems.at[1]),
        ]
        for copy in copies:
            copy.start()
        for copy in copies:
            copy.wait()
        row[...] = jnp.full(row.shape, rates[order[lax.axis_index("ckpt")]], jnp.float32)

    return call(
        kernel,
        "rate_row",
        [jax.ShapeDtypeStruct((1, columns), jnp.float32)],
        [ANY, ANY],
        (learn_rates, ckpt_order),
        scratch=[
            pltpu.SMEM(learn_rates.shape, learn_rates.dtype),
            pltpu.SMEM(ckpt_order.shape, ckpt_order.dtype),
            pltpu.SemaphoreType.DMA((2,)),
        ],
    )[0]


def score(blocks, train, sums, rate, forward):
    count = len(blocks)
    rows, width = blocks[0].shape
    args = [*blocks, train, *(sums or ()), *(() if rate is None else (rate,))]

    def kernel(*refs):
        given, train_ref, before = refs[:count], refs[count], refs[count + 1 : len(args)]
        outs = refs[len(args) :]
        stacked = given[0][...] if count == 1 else jnp.concatenate([ref[...] for ref in given], axis=0)
        scores = times(stacked, train_ref[...])
        for i in range(count):
            total = scores[i * rows : (i + 1) * rows]
            if sums:
                total = before[i][...] + total
            if rate is not None:
                total = total * before[-1][...]
            outs[i][...] = total

    shapes = [jax.ShapeDtypeStruct((rows, train.shape[0]), jnp.float32)] * count
    aliases = {}
    if forward:
        shapes.append(jax.ShapeDtypeStruct(blocks[-1].shape, blocks[-1].dtype))
        aliases[count - 1] = count
    results = call(
        kernel, "score", shapes, [VMEM] * len(args), args, flops=2 * 256 * width * train.shape[0], aliases=aliases
    )
    return list(results[:count]), results[count] if forward else None


def sort_out(sums, shards, groups, after):
    per_group = shards // groups
    rows, columns = sums[0].shape

    def kernel(after_ref, *refs):
        given, outs = refs[: len(sums)], refs[len(sums) :]
        my_place = ring_position(lax.axis_index("shard"), shards)
        my_group = lax.axis_index("ckpt") * lax.axis_size("sub") + lax.axis_index("sub")
        for d in range(groups):
            out = outs[1 - d % 2]
            for k in range(per_group):
                chip = (my_group ^ d) * per_group + k
                step = (my_place - ring_position(chip, shards) + shards) % shards
                at = pl.ds((d // 2 * per_group + k) * rows, rows)

                @pl.when(step == shards - 1)
                def _():
                    out[at, :] = jnp.zeros((rows, columns), jnp.float32)

                for s, ref in enumerate(given):

                    @pl.when(step == s)
                    def _():
                        out[at, :] = ref[...]

    shape = jax.ShapeDtypeStruct((groups // 2 * per_group * rows, columns), jnp.float32)
    return call(kernel, "sort_out", [shape] * 2, [ANY] + [VMEM] * len(sums), (after, *sums))


def fold(kept, received, tall):
    pieces = kept.shape[0] // tall

    def kernel(kept_ref, received_ref, *outs):
        if pieces == 1:
            outs[0][...] = kept_ref[...] + received_ref[...]
            return
        for i in range(pieces):
            at = pl.ds(i * tall, tall)
            outs[1 - i % 2][pl.ds(i // 2 * tall, tall), :] = kept_ref[at, :] + received_ref[at, :]

    shapes = [jax.ShapeDtypeStruct((max(pieces // 2, 1) * tall, kept.shape[1]), jnp.float32)] * min(pieces, 2)
    return call(kernel, "fold", shapes, [VMEM] * 2, (kept, received))


def finish(result, last, received, shards, groups):
    per_group = shards // groups
    rows = last.shape[0]

    def kernel(result_ref, last_ref, received_ref, out):
        my_place = ring_position(lax.axis_index("shard"), shards)
        my_group = lax.axis_index("ckpt") * lax.axis_size("sub") + lax.axis_index("sub")
        last_chip = chip_at((my_place + 1) % shards, shards)
        mine = last_chip // per_group == my_group
        out[...] = result_ref[...]

        @pl.when(mine)
        def _():
            at = pl.ds(pl.multiple_of(last_chip % per_group * rows, rows), rows) if per_group > 1 else slice(None)
            out[at, :] += last_ref[...] + received_ref[...]

    return call(
        kernel,
        "finish",
        [jax.ShapeDtypeStruct(result.shape, jnp.float32)],
        [VMEM] * 3,
        (result, last, received),
    )[0]


def per_device(sizes, train_grads, query_grads, precond, learn_rates, ckpt_order):
    train_local = train_grads[0]
    query_local = query_grads[0]
    parts, shards, ckpts, subs = sizes
    groups = ckpts * subs
    per_group = shards // groups
    ring = line_ring(shards)
    place = {z: i for i, z in enumerate(ring)}
    hops = [(ring[i], ring[(i + 1) % shards]) for i in range(shards)]

    unit = query_local.shape[1] // sum(CHUNKS)
    spans = [(unit * sum(CHUNKS[:j]), unit * c) for j, c in enumerate(CHUNKS)]
    query_local = pltpu.with_memory_space_constraint(query_local, pltpu.HBM)
    precond = pltpu.with_memory_space_constraint(precond, pltpu.HBM)
    train_local = pltpu.with_memory_space_constraint(train_local, pltpu.HBM)
    own = condition(query_local, precond, spans[:1]) + condition(query_local, precond, spans[1:])
    held = [fetch(train_local, span) for span in spans]
    rate = rate_row(
        pltpu.with_memory_space_constraint(learn_rates, pltpu.HBM),
        pltpu.with_memory_space_constraint(ckpt_order, pltpu.HBM),
        train_local.shape[0],
    )

    sums = []
    current = own
    for step in range(1, shards):
        current = [lax.ppermute(block, "shard", hops) for block in current]
        if step == shards - 1:
            sent, kept = sort_out(sums, shards, groups, current[0])
        total = None
        for j in range(len(CHUNKS)):
            total, current[j] = score(
                [own[j], current[j]] if step == 1 else [current[j]],
                held[j],
                total,
                rate if j == len(CHUNKS) - 1 else None,
                step < shards - 1,
            )
        sums += total

    def last_of(z):
        return ring[(place[z] + 1) % shards]

    def device(p, z, g):
        return ((p * shards + z) * ckpts + g // subs) * subs + g % subs

    def pairs(d, keep):
        return [
            (device(p, z, g), device(p, z, g ^ d))
            for p in range(parts)
            for z in range(shards)
            for g in range(groups)
            if keep(z, g ^ d)
        ]

    distances = [1 << i for i in range(groups.bit_length() - 1)]
    tall = kept.shape[0] // (groups // 2)
    for d in distances:
        received = lax.ppermute(sent, AXES, pairs(d, lambda z, g: True))
        *more, kept = fold(kept, received, tall)
        sent = more[0] if more else None

    last = sums[-1]
    for d in distances:
        received = lax.ppermute(
            last,
            AXES,
            pairs(d, lambda z, g: (last_of(z) // per_group ^ g) & (2 * d - 1) == 0),
        )
        if d < groups // 2:
            last = fold(last, received, last.shape[0])[0]
    return finish(kept, last, received, shards, groups)


def solution(mesh):
    sizes = tuple(mesh.shape[a] for a in AXES)

    def run(*args):
        return per_device(sizes, *args)

    return jax.shard_map(
        run,
        mesh=mesh,
        in_specs=(
            P("ckpt", ("parts", "shard"), "sub"),
            P("ckpt", ("parts", "shard"), "sub"),
            P("ckpt", "sub"),
            P(),
            P(),
        ),
        out_specs=P(("ckpt", "sub"), ("parts", "shard")),
        check_vma=False,
    )
```

```python
import jax
import jax.numpy as jnp
from jax import lax
from jax.experimental import pallas as pl
from jax.experimental.pallas import tpu as pltpu
from jax.sharding import PartitionSpec as P

CHUNKS = (6, 6, 4)
QUARTERS = (4, 4, 4, 4)
VMEM = pl.BlockSpec(memory_space=pltpu.VMEM)
SMEM = pl.BlockSpec(memory_space=pltpu.SMEM)
HBM = pl.BlockSpec(memory_space=pltpu.HBM)
ANY = pl.BlockSpec(memory_space=pl.ANY)
PIECES = 4
SCALE = 0.1


def line_ring(n):
    odd = list(range(1, n, 2))
    even = list(range(0, n, 2))
    return [0] + odd + even[:0:-1]


def ring_position(z, n):
    return jnp.where(z == 0, 0, jnp.where(z % 2 == 1, (z + 1) // 2, n - z // 2))


def call(kernel, name, shapes, specs, args, limit=8, scratch=(), flops=0, aliases=None, after=()):
    args = (*args, *after)
    specs = [*specs, *[ANY] * len(after)]
    count = len(args) - len(after)

    def body(*refs):
        kernel(*refs[:count], *refs[len(args) :])

    return pl.pallas_call(
        body,
        in_specs=specs,
        out_specs=[VMEM] * len(shapes),
        out_shape=shapes,
        scratch_shapes=scratch,
        input_output_aliases=aliases or {},
        compiler_params=pltpu.CompilerParams(vmem_limit_bytes=limit << 20),
        cost_estimate=pl.CostEstimate(flops=int(SCALE * flops), bytes_accessed=0, transcendentals=0),
        name=name,
    )(*args)


def times(rows, train_part):
    return lax.dot_general(
        rows, train_part, (((1,), (1,)), ((), ())), preferred_element_type=jnp.float32
    )


def condition(query, precond, spans, after=()):
    rows = query.shape[0]
    count = len(spans)
    first, total = spans[0][0], sum(width for _, width in spans)

    def kernel(query_ref, precond_ref, *refs):
        outs, (held, scale, sems) = refs[:count], refs[count:]
        copies = [pltpu.make_async_copy(precond_ref.at[:, pl.ds(first, total)], scale, sems.at[count])]
        copies += [
            pltpu.make_async_copy(
                query_ref.at[:, pl.ds(start, width)], held.at[:, pl.ds(start - first, width)], sems.at[i]
            )
            for i, (start, width) in enumerate(spans)
        ]
        for copy in copies:
            copy.start()
        copies[0].wait()
        for i, (start, width) in enumerate(spans):
            copies[i + 1].wait()
            at = pl.ds(start - first, width)
            outs[i][...] = (held[:, at] * scale[:, at]).astype(jnp.bfloat16)

    return call(
        kernel,
        "condition",
        [jax.ShapeDtypeStruct((rows, width), jnp.bfloat16) for _, width in spans],
        [HBM, HBM],
        (query, precond),
        scratch=[
            pltpu.VMEM((rows, total), jnp.float32),
            pltpu.VMEM((1, total), jnp.float32),
            pltpu.SemaphoreType.DMA((count + 1,)),
        ],
        after=after,
    )


def fetch(train, spans, after):
    count = train.shape[0]
    tall = count // PIECES

    def kernel(train_ref, *refs):
        outs, sems = refs[:-1], refs[-1]
        copies = [
            pltpu.make_async_copy(
                train_ref.at[pl.ds(i * tall, tall), pl.ds(start, width)],
                out.at[pl.ds(i * tall, tall), :],
                sems.at[k, i],
            )
            for k, (out, (start, width)) in enumerate(zip(outs, spans))
            for i in range(PIECES)
        ]
        for copy in copies:
            copy.start()
        for copy in copies:
            copy.wait()

    return call(
        kernel,
        "fetch",
        [pltpu.VMEM((count, width), train.dtype) for _, width in spans],
        [ANY],
        (train,),
        scratch=[pltpu.SemaphoreType.DMA((len(spans), PIECES))],
        flops=2 * 512 * sum(width for _, width in spans) * count,
        after=after,
    )


def rate_row(learn_rates, ckpt_order, columns, after):
    def kernel(rates_ref, order_ref, row, rates, order, sems):
        copies = [
            pltpu.make_async_copy(rates_ref, rates, sems.at[0]),
            pltpu.make_async_copy(order_ref, order, sems.at[1]),
        ]
        for copy in copies:
            copy.start()
        for copy in copies:
            copy.wait()
        row[...] = jnp.full(row.shape, rates[order[lax.axis_index("ckpt")]], jnp.float32)

    return call(
        kernel,
        "rate_row",
        [jax.ShapeDtypeStruct((1, columns), jnp.float32)],
        [ANY, ANY],
        (learn_rates, ckpt_order),
        scratch=[
            pltpu.SMEM(learn_rates.shape, learn_rates.dtype),
            pltpu.SMEM(ckpt_order.shape, ckpt_order.dtype),
            pltpu.SemaphoreType.DMA((2,)),
        ],
        after=after,
    )[0]


def score(blocks, train, sums, forward=False, carry=None, after=()):
    count = len(blocks)
    rows, width = blocks[0].shape
    args = [*blocks, train, *(sums or ())]
    specs = [VMEM] * len(args)

    def kernel(*refs):
        given, train_ref, before = refs[:count], refs[count], refs[count + 1 : len(args)]
        outs = refs[-count:] if carry is None else refs[-count - 1 : -1]
        outs = outs if not forward else refs[-count - 1 : -1]
        stacked = given[0][...] if count == 1 else jnp.concatenate([ref[...] for ref in given], axis=0)
        scores = times(stacked, train_ref[...])
        for i in range(count):
            total = scores[i * rows : (i + 1) * rows]
            if sums:
                total = before[i][...] + total
            outs[i][...] = total

    shapes = [jax.ShapeDtypeStruct((rows, train.shape[0]), jnp.float32)] * count
    aliases = {}
    if forward:
        shapes.append(jax.ShapeDtypeStruct(blocks[-1].shape, blocks[-1].dtype))
        aliases[count - 1] = count
    elif carry is not None:
        shapes.append(jax.ShapeDtypeStruct(carry.shape, carry.dtype))
        aliases[len(args)] = count
        args.append(carry)
        specs.append(ANY)
    results = call(
        kernel,
        "score",
        shapes,
        specs,
        args,
        flops=2 * 256 * width * train.shape[0],
        aliases=aliases,
        after=after,
    )
    return list(results[:count]), results[count] if len(shapes) > count else None


def sort_out(sums, rate, shards, groups):
    per_group = shards // groups
    rows, columns = sums[0].shape

    def kernel(*refs):
        given, rate_ref, outs = refs[: len(sums)], refs[len(sums)], refs[len(sums) + 1 :]
        my_place = ring_position(lax.axis_index("shard"), shards)
        my_group = lax.axis_index("ckpt") * lax.axis_size("sub") + lax.axis_index("sub")
        for d in range(groups):
            for k in range(per_group):
                chip = (my_group ^ d) * per_group + k
                step = (my_place - ring_position(chip, shards) + shards) % shards
                at = pl.ds((d // 2 * per_group + k) * rows, rows)
                for s, ref in enumerate(given):

                    @pl.when(step == s)
                    def _():
                        outs[1 - d % 2][at, :] = ref[...] * rate_ref[...]

    shape = jax.ShapeDtypeStruct((groups // 2 * per_group * rows, columns), jnp.float32)
    return call(kernel, "sort_out", [shape] * 2, [VMEM] * (len(sums) + 1), (*sums, rate))


def fold(kept, received, tall):
    pieces = kept.shape[0] // tall

    def kernel(kept_ref, received_ref, *outs):
        if pieces == 1:
            outs[0][...] = kept_ref[...] + received_ref[...]
            return
        for i in range(pieces):
            at = pl.ds(i * tall, tall)
            outs[1 - i % 2][pl.ds(i // 2 * tall, tall), :] = kept_ref[at, :] + received_ref[at, :]

    shapes = [jax.ShapeDtypeStruct((max(pieces // 2, 1) * tall, kept.shape[1]), jnp.float32)] * min(pieces, 2)
    return call(kernel, "fold", shapes, [VMEM] * 2, (kept, received))


def my_pair():
    z = lax.axis_index("shard")
    return z // 2 == lax.axis_index("ckpt"), z % 2 == lax.axis_index("sub")


def score_and_deal(own, far, train, sums, after):
    rows, width = own.shape
    args = [own, far, train, *(sums or ())]

    def kernel(own_ref, far_ref, train_ref, *refs):
        before, (own_sums, far_sums, first, second) = refs[:-4], refs[-4:]
        scores = times(jnp.concatenate([own_ref[...], far_ref[...]], axis=0), train_ref[...])
        for i, out in enumerate((own_sums, far_sums)):
            part = scores[i * rows : (i + 1) * rows]
            out[...] = before[i][...] + part if sums else part
        home, _ = my_pair()

        @pl.when(home)
        def _():
            first[...] = far_ref[...]
            second[...] = own_ref[...]

        @pl.when(jnp.logical_not(home))
        def _():
            first[...] = own_ref[...]
            second[...] = far_ref[...]

    scores = jax.ShapeDtypeStruct((rows, train.shape[0]), jnp.float32)
    block = jax.ShapeDtypeStruct(own.shape, own.dtype)
    return call(
        kernel,
        "score_and_deal",
        [scores, scores, block, block],
        [VMEM] * len(args),
        args,
        flops=2 * 256 * width * train.shape[0],
        after=after,
    )


def score_picked(block, train, if_home, if_not, carry=None, after=()):
    rows, width = block.shape
    args = [block, train, if_home, if_not]

    def kernel(block_ref, train_ref, home_ref, not_ref, *refs):
        out = refs[0] if carry is None else refs[1]
        part = times(block_ref[...], train_ref[...])
        home, _ = my_pair()

        @pl.when(home)
        def _():
            out[...] = home_ref[...] + part

        @pl.when(jnp.logical_not(home))
        def _():
            out[...] = not_ref[...] + part

    scores = jax.ShapeDtypeStruct((rows, train.shape[0]), jnp.float32)
    flops = 2 * 256 * width * train.shape[0]
    if carry is None:
        return call(kernel, "score_picked", [scores], [VMEM] * 4, args, flops=flops, after=after)[0]
    return call(
        kernel,
        "score_picked",
        [scores, jax.ShapeDtypeStruct(carry.shape, carry.dtype)],
        [VMEM] * 4 + [ANY],
        [*args, carry],
        flops=flops,
        after=after,
        aliases={4: 1},
    )


def part_pair(if_home, if_not, other, rate, after=()):
    def kernel(home_ref, not_ref, other_ref, rate_ref, sent, kept):
        home, agree = my_pair()
        for one, ref in ((home, home_ref), (jnp.logical_not(home), not_ref)):

            @pl.when(jnp.logical_and(one, agree))
            def _():
                kept[...] = ref[...] * rate_ref[...]
                sent[...] = other_ref[...] * rate_ref[...]

            @pl.when(jnp.logical_and(one, jnp.logical_not(agree)))
            def _():
                sent[...] = ref[...] * rate_ref[...]
                kept[...] = other_ref[...] * rate_ref[...]

    shape = jax.ShapeDtypeStruct(other.shape, jnp.float32)
    return call(kernel, "part_pair", [shape] * 2, [VMEM] * 4, (if_home, if_not, other, rate), after=after)


def add(*arrays):
    def kernel(*refs):
        total = refs[0][...]
        for ref in refs[1:-1]:
            total = total + ref[...]
        refs[-1][...] = total

    shape = jax.ShapeDtypeStruct(arrays[0].shape, jnp.float32)
    return call(kernel, "add", [shape], [VMEM] * len(arrays), arrays)[0]


def in_pairs(train, query, precond, learn_rates, ckpt_order):
    def swap(array, axis, distance):
        size = lax.axis_size(axis)
        return lax.ppermute(array, axis, [(i, i ^ distance) for i in range(size)])

    unit = query.shape[1] // sum(QUARTERS)
    spans = [(unit * sum(QUARTERS[:j]), unit * c) for j, c in enumerate(QUARTERS)]

    own1 = condition(query, precond, spans[:1])[0]
    one1, two1 = swap(own1, "shard", 1), swap(own1, "shard", 2)
    own2 = condition(query, precond, spans[1:2], [own1])[0]
    one2, two2 = swap(own2, "shard", 1), swap(own2, "shard", 2)
    train1, train2 = fetch(train, spans[:2], [own2])
    totals, two1 = score([own1, one1, two1], train1, None, forward=True)
    three1 = swap(two1, "shard", 1)
    own3, own4 = condition(query, precond, spans[2:], totals[:1])
    two3 = swap(own3, "shard", 2)
    totals, two2 = score([own2, one2, two2], train2, totals, forward=True, after=[own3])
    three2 = swap(two2, "shard", 1)
    own_sums, one_sums, two_sums = totals
    two4 = swap(own4, "shard", 2)
    train3, train4 = fetch(train, spans[2:], totals[:1])
    (three_sums,), _ = score([three1], train1, None, after=[train3])

    own_sums, two_sums, first3, second3 = score_and_deal(own3, two3, train3, [own_sums, two_sums], [three_sums])
    first3 = swap(first3, "shard", 1)
    own_sums, two_sums, first4, second4 = score_and_deal(own4, two4, train4, [own_sums, two_sums], [])
    first4 = swap(first4, "shard", 1)
    (three_sums,), second3 = score([three2], train2, [three_sums], carry=second3, after=[own_sums])
    second3 = swap(second3, "shard", 1)
    rate = rate_row(learn_rates, ckpt_order, train.shape[0], [three_sums])
    first_sums, second4 = score_picked(first3, train3, three_sums, one_sums, second4, [rate])
    second4 = swap(second4, "shard", 1)
    first_sums = score_picked(first4, train4, first_sums, first_sums)

    sent, kept = part_pair(two_sums, own_sums, first_sums, rate)
    across = add(kept, swap(sent, "sub", 1))
    from_far = swap(across, "ckpt", 1)
    second_sums = score_picked(second3, train3, one_sums, three_sums, after=[across])
    second_sums = score_picked(second4, train4, second_sums, second_sums)
    sent, kept = part_pair(own_sums, two_sums, second_sums, rate)
    return add(kept, from_far, swap(sent, "sub", 1))


def in_ring(sizes, train_local, query_local, precond, learn_rates, ckpt_order):
    shards, groups = sizes[0], sizes[1] * sizes[2]
    ring = line_ring(shards)
    hops = [(ring[i], ring[(i + 1) % shards]) for i in range(shards)]

    unit = query_local.shape[1] // sum(CHUNKS)
    spans = [(unit * sum(CHUNKS[:j]), unit * c) for j, c in enumerate(CHUNKS)]
    own = condition(query_local, precond, spans[:1])
    held = fetch(train_local, spans[:1], own)
    for span in spans[1:]:
        own += condition(query_local, precond, [span], [held[0], own[-1]])

    sums = []
    current = own
    for step in range(1, shards):
        current = [lax.ppermute(block, "shard", hops) for block in current]
        total = None
        for j in range(len(CHUNKS)):
            if j >= len(held):
                held += fetch(train_local, spans[j : j + 1], total[:1])
            total, current[j] = score(
                [own[j], current[j]] if step == 1 else [current[j]], held[j], total, step < shards - 1
            )
        sums += total
    rate = rate_row(learn_rates, ckpt_order, train_local.shape[0], sums[:1])

    sent, kept = sort_out(sums, rate, shards, groups)
    tall = kept.shape[0] // (groups // 2)
    for i in range(groups.bit_length() - 1):
        received = lax.ppermute(sent, ("ckpt", "sub"), [(g, g ^ 1 << i) for g in range(groups)])
        *more, kept = fold(kept, received, tall)
        sent = more[0] if more else None
    return kept


def per_device(sizes, train_grads, query_grads, precond, learn_rates, ckpt_order):
    args = [train_grads[0], query_grads[0], precond, learn_rates, ckpt_order]
    args = [pltpu.with_memory_space_constraint(array, pltpu.HBM) for array in args]
    return in_pairs(*args) if sizes == (4, 2, 2) else in_ring(sizes, *args)


def solution(mesh):
    sizes = tuple(mesh.shape[axis] for axis in ("shard", "ckpt", "sub"))

    def run(*args):
        return per_device(sizes, *args)

    return jax.shard_map(
        run,
        mesh=mesh,
        in_specs=(
            P("ckpt", ("parts", "shard"), "sub"),
            P("ckpt", ("parts", "shard"), "sub"),
            P("ckpt", "sub"),
            P(),
            P(),
        ),
        out_specs=P(("ckpt", "sub"), ("parts", "shard")),
        check_vma=False,
    )
```

```python
import jax
import jax.numpy as jnp
from jax import lax
from jax.experimental import pallas as pl
from jax.experimental.pallas import tpu as pltpu
from jax.sharding import PartitionSpec as P

CHUNKS = (6, 6, 4)
QUARTERS = (4, 4, 4, 4)
VMEM = pl.BlockSpec(memory_space=pltpu.VMEM)
SMEM = pl.BlockSpec(memory_space=pltpu.SMEM)
HBM = pl.BlockSpec(memory_space=pltpu.HBM)
ANY = pl.BlockSpec(memory_space=pl.ANY)
PIECES = 4
SCALE = 0.1


def line_ring(n):
    odd = list(range(1, n, 2))
    even = list(range(0, n, 2))
    return [0] + odd + even[:0:-1]


def ring_position(z, n):
    return jnp.where(z == 0, 0, jnp.where(z % 2 == 1, (z + 1) // 2, n - z // 2))


def call(kernel, name, shapes, specs, args, limit=8, scratch=(), flops=0, aliases=None, after=()):
    args = (*args, *after)
    specs = [*specs, *[ANY] * len(after)]
    count = len(args) - len(after)

    def body(*refs):
        kernel(*refs[:count], *refs[len(args) :])

    return pl.pallas_call(
        body,
        in_specs=specs,
        out_specs=[VMEM] * len(shapes),
        out_shape=shapes,
        scratch_shapes=scratch,
        input_output_aliases=aliases or {},
        compiler_params=pltpu.CompilerParams(vmem_limit_bytes=limit << 20),
        cost_estimate=pl.CostEstimate(flops=int(SCALE * flops), bytes_accessed=0, transcendentals=0),
        name=name,
    )(*args)


def times(rows, train_part):
    return lax.dot_general(
        rows, train_part, (((1,), (1,)), ((), ())), preferred_element_type=jnp.float32
    )


def fetch(train, spans, after=(), query=None, precond=None, query_spans=()):
    count = train.shape[0]
    tall = count // PIECES
    made = len(query_spans)
    first, total = (query_spans[0][0], sum(width for _, width in query_spans)) if made else (0, 0)

    def kernel(train_ref, *refs):
        copies = []
        if made:
            query_ref, precond_ref, *refs, held, scale, query_sems = refs
            copies.append(pltpu.make_async_copy(precond_ref.at[:, pl.ds(first, total)], scale, query_sems.at[made]))
            copies += [
                pltpu.make_async_copy(
                    query_ref.at[:, pl.ds(start, width)], held.at[:, pl.ds(start - first, width)], query_sems.at[i]
                )
                for i, (start, width) in enumerate(query_spans)
            ]
        blocks, outs, sems = refs[:made], refs[made:-1], refs[-1]
        for copy in copies:
            copy.start()
        train_copies = [
            pltpu.make_async_copy(
                train_ref.at[pl.ds(i * tall, tall), pl.ds(start, width)],
                out.at[pl.ds(i * tall, tall), :],
                sems.at[k, i],
            )
            for k, (out, (start, width)) in enumerate(zip(outs, spans))
            for i in range(PIECES)
        ]
        for copy in train_copies:
            copy.start()
        if made:
            copies[0].wait()
        for i, (start, width) in enumerate(query_spans):
            copies[i + 1].wait()
            at = pl.ds(start - first, width)
            blocks[i][...] = (held[:, at] * scale[:, at]).astype(jnp.bfloat16)
        for copy in train_copies:
            copy.wait()

    rows = query.shape[0] if made else 0
    scratch = [pltpu.SemaphoreType.DMA((max(len(spans), 1), PIECES))]
    if made:
        scratch += [
            pltpu.VMEM((rows, total), jnp.float32),
            pltpu.VMEM((1, total), jnp.float32),
            pltpu.SemaphoreType.DMA((made + 1,)),
        ]
    shapes = [jax.ShapeDtypeStruct((rows, width), jnp.bfloat16) for _, width in query_spans]
    shapes += [pltpu.VMEM((count, width), train.dtype) for _, width in spans]
    return call(
        kernel,
        "fetch" if spans else "condition",
        shapes,
        [ANY] * (3 if made else 1),
        (train, query, precond) if made else (train,),
        scratch=scratch,
        flops=2 * 512 * sum(width for _, width in spans) * count,
        after=after,
    )


def rate_row(learn_rates, ckpt_order, columns, after):
    def kernel(rates_ref, order_ref, row, rates, order, sems):
        copies = [
            pltpu.make_async_copy(rates_ref, rates, sems.at[0]),
            pltpu.make_async_copy(order_ref, order, sems.at[1]),
        ]
        for copy in copies:
            copy.start()
        for copy in copies:
            copy.wait()
        row[...] = jnp.full(row.shape, rates[order[lax.axis_index("ckpt")]], jnp.float32)

    return call(
        kernel,
        "rate_row",
        [jax.ShapeDtypeStruct((1, columns), jnp.float32)],
        [ANY, ANY],
        (learn_rates, ckpt_order),
        scratch=[
            pltpu.SMEM(learn_rates.shape, learn_rates.dtype),
            pltpu.SMEM(ckpt_order.shape, ckpt_order.dtype),
            pltpu.SemaphoreType.DMA((2,)),
        ],
        after=after,
    )[0]


def score(blocks, train, sums=(), picked=(), forward=False, after=()):
    count = len(blocks)
    rows, width = blocks[0].shape
    args = [*blocks, train, *sums, *picked]

    def kernel(*refs):
        given, train_ref, before, outs = refs[:count], refs[count], refs[count + 1 : len(args)], refs[len(args) :]
        stacked = given[0][...] if count == 1 else jnp.concatenate([ref[...] for ref in given], axis=0)
        scores = times(stacked, train_ref[...])
        for i in range(count):
            part = scores[i * rows : (i + 1) * rows]
            if i < len(sums):
                outs[i][...] = before[i][...] + part
            elif picked:
                home, _ = my_pair()

                @pl.when(home)
                def _():
                    outs[i][...] = before[-2][...] + part

                @pl.when(jnp.logical_not(home))
                def _():
                    outs[i][...] = before[-1][...] + part
            else:
                outs[i][...] = part

    shapes = [jax.ShapeDtypeStruct((rows, train.shape[0]), jnp.float32)] * count
    if forward:
        shapes.append(jax.ShapeDtypeStruct(blocks[-1].shape, blocks[-1].dtype))
    return call(
        kernel,
        "score",
        shapes,
        [VMEM] * len(args),
        args,
        flops=2 * 256 * width * train.shape[0],
        aliases={count - 1: count} if forward else None,
        after=after,
    )


def sort_out(sums, rate, shards, groups):
    per_group = shards // groups
    rows, columns = sums[0].shape

    def kernel(*refs):
        given, rate_ref, outs = refs[: len(sums)], refs[len(sums)], refs[len(sums) + 1 :]
        my_place = ring_position(lax.axis_index("shard"), shards)
        my_group = lax.axis_index("ckpt") * lax.axis_size("sub") + lax.axis_index("sub")
        for d in range(groups):
            for k in range(per_group):
                chip = (my_group ^ d) * per_group + k
                step = (my_place - ring_position(chip, shards) + shards) % shards
                at = pl.ds((d // 2 * per_group + k) * rows, rows)
                for s, ref in enumerate(given):

                    @pl.when(step == s)
                    def _():
                        outs[1 - d % 2][at, :] = ref[...] * rate_ref[...]

    shape = jax.ShapeDtypeStruct((groups // 2 * per_group * rows, columns), jnp.float32)
    return call(kernel, "sort_out", [shape] * 2, [VMEM] * (len(sums) + 1), (*sums, rate))


def fold(kept, received, tall):
    pieces = kept.shape[0] // tall

    def kernel(kept_ref, received_ref, *outs):
        if pieces == 1:
            outs[0][...] = kept_ref[...] + received_ref[...]
            return
        for i in range(pieces):
            at = pl.ds(i * tall, tall)
            outs[1 - i % 2][pl.ds(i // 2 * tall, tall), :] = kept_ref[at, :] + received_ref[at, :]

    shapes = [jax.ShapeDtypeStruct((max(pieces // 2, 1) * tall, kept.shape[1]), jnp.float32)] * min(pieces, 2)
    return call(kernel, "fold", shapes, [VMEM] * 2, (kept, received))


def my_pair():
    z = lax.axis_index("shard")
    return z // 2 == lax.axis_index("ckpt"), z % 2 == lax.axis_index("sub")


def deal(own, far, after=()):
    def kernel(own_ref, far_ref, first, second):
        home, _ = my_pair()

        @pl.when(home)
        def _():
            first[...] = far_ref[...]
            second[...] = own_ref[...]

        @pl.when(jnp.logical_not(home))
        def _():
            first[...] = own_ref[...]
            second[...] = far_ref[...]

    shape = jax.ShapeDtypeStruct(own.shape, own.dtype)
    return call(kernel, "deal", [shape] * 2, [VMEM] * 2, (own, far), after=after)


def hand_on(array, after):
    def kernel(_, __):
        pass

    shape = jax.ShapeDtypeStruct(array.shape, array.dtype)
    return call(kernel, "hand_on", [shape], [VMEM], (array,), after=after, aliases={0: 0})[0]


def part_pair(if_home, if_not, other, rate, after=()):
    def kernel(home_ref, not_ref, other_ref, rate_ref, sent, kept):
        home, agree = my_pair()
        for one, ref in ((home, home_ref), (jnp.logical_not(home), not_ref)):

            @pl.when(jnp.logical_and(one, agree))
            def _():
                kept[...] = ref[...] * rate_ref[...]
                sent[...] = other_ref[...] * rate_ref[...]

            @pl.when(jnp.logical_and(one, jnp.logical_not(agree)))
            def _():
                sent[...] = ref[...] * rate_ref[...]
                kept[...] = other_ref[...] * rate_ref[...]

    shape = jax.ShapeDtypeStruct(other.shape, jnp.float32)
    return call(kernel, "part_pair", [shape] * 2, [VMEM] * 4, (if_home, if_not, other, rate), after=after)


def add(*arrays):
    def kernel(*refs):
        total = refs[0][...]
        for ref in refs[1:-1]:
            total = total + ref[...]
        refs[-1][...] = total

    shape = jax.ShapeDtypeStruct(arrays[0].shape, jnp.float32)
    return call(kernel, "add", [shape], [VMEM] * len(arrays), arrays)[0]


def in_pairs(train, query, precond, learn_rates, ckpt_order):
    def swap(array, axis, distance):
        size = lax.axis_size(axis)
        return lax.ppermute(array, axis, [(i, i ^ distance) for i in range(size)])

    unit = query.shape[1] // sum(QUARTERS)
    spans = [(unit * sum(QUARTERS[:j]), unit * c) for j, c in enumerate(QUARTERS)]

    (own1,) = fetch(train, [], [], query, precond, spans[:1])
    two1 = swap(own1, "shard", 2)
    one1 = swap(own1, "shard", 1)
    (own2,) = fetch(train, [], [own1], query, precond, spans[1:2])
    two2 = swap(own2, "shard", 2)
    one2 = swap(own2, "shard", 1)
    own3, own4, train1, train2, train3, train4 = fetch(train, spans, [own2], query, precond, spans[2:])
    two3 = swap(own3, "shard", 2)
    two4 = swap(own4, "shard", 2)
    two1 = hand_on(two1, [own4, one1])
    three1 = swap(two1, "shard", 1)
    two2 = hand_on(two2, [two1, one2])
    three2 = swap(two2, "shard", 1)

    sums = score([own1, one1, two1, three1], train1, after=[two2])
    first3, second3 = deal(own3, two3, [sums[0]])
    first3 = swap(first3, "shard", 1)
    sums = score([own2, one2, two2, three2], train2, sums, after=[second3])
    first4, second4 = deal(own4, two4, [sums[0]])
    first4 = swap(first4, "shard", 1)
    own_sums, one_sums, two_sums, three_sums = sums
    rate = rate_row(learn_rates, ckpt_order, train.shape[0], [second4])
    second3 = swap(hand_on(second3, [first3, rate]), "shard", 1)
    own_sums, two_sums, first_sums = score(
        [own3, two3, first3], train3, [own_sums, two_sums], (three_sums, one_sums), after=[second4]
    )
    second4 = swap(hand_on(second4, [own_sums]), "shard", 1)
    own_sums, two_sums, first_sums = score([own4, two4, first4], train4, [own_sums, two_sums, first_sums])

    sent, kept = part_pair(two_sums, own_sums, first_sums, rate)
    across = add(kept, swap(sent, "sub", 1))
    from_far = swap(across, "ckpt", 1)
    (second_sums,) = score([second3], train3, picked=(one_sums, three_sums), after=[across])
    (second_sums,) = score([second4], train4, [second_sums])
    sent, kept = part_pair(own_sums, two_sums, second_sums, rate)
    return add(kept, from_far, swap(sent, "sub", 1))


def in_ring(sizes, train_local, query_local, precond, learn_rates, ckpt_order):
    shards, groups = sizes[0], sizes[1] * sizes[2]
    ring = line_ring(shards)
    hops = [(ring[i], ring[(i + 1) % shards]) for i in range(shards)]

    unit = query_local.shape[1] // sum(CHUNKS)
    spans = [(unit * sum(CHUNKS[:j]), unit * c) for j, c in enumerate(CHUNKS)]
    own = fetch(train_local, [], [], query_local, precond, spans[:1])
    held = fetch(train_local, spans[:1], own)
    for span in spans[1:]:
        own += fetch(train_local, [], [held[0], own[-1]], query_local, precond, [span])

    sums = []
    current = own
    for step in range(1, shards):
        current = [lax.ppermute(block, "shard", hops) for block in current]
        forward = step < shards - 1
        total = ()
        for j in range(len(CHUNKS)):
            if j >= len(held):
                held += fetch(train_local, spans[j : j + 1], total[:1])
            blocks = [own[j], current[j]] if step == 1 else [current[j]]
            total = score(blocks, held[j], total, forward=forward)
            if forward:
                *total, current[j] = total
        sums += total
    rate = rate_row(learn_rates, ckpt_order, train_local.shape[0], sums[:1])

    sent, kept = sort_out(sums, rate, shards, groups)
    tall = kept.shape[0] // (groups // 2)
    for i in range(groups.bit_length() - 1):
        received = lax.ppermute(sent, ("ckpt", "sub"), [(g, g ^ 1 << i) for g in range(groups)])
        *more, kept = fold(kept, received, tall)
        sent = more[0] if more else None
    return kept


def per_device(sizes, train_grads, query_grads, precond, learn_rates, ckpt_order):
    args = [train_grads[0], query_grads[0], precond, learn_rates, ckpt_order]
    args = [pltpu.with_memory_space_constraint(array, pltpu.HBM) for array in args]
    return in_pairs(*args) if sizes == (4, 2, 2) else in_ring(sizes, *args)


def solution(mesh):
    sizes = tuple(mesh.shape[axis] for axis in ("shard", "ckpt", "sub"))

    def run(*args):
        return per_device(sizes, *args)

    return jax.shard_map(
        run,
        mesh=mesh,
        in_specs=(
            P("ckpt", ("parts", "shard"), "sub"),
            P("ckpt", ("parts", "shard"), "sub"),
            P("ckpt", "sub"),
            P(),
            P(),
        ),
        out_specs=P(("ckpt", "sub"), ("parts", "shard")),
        check_vma=False,
    )
```

```python
import jax
import jax.numpy as jnp
from jax import lax
from jax.experimental import pallas as pl
from jax.experimental.pallas import tpu as pltpu
from jax.sharding import PartitionSpec as P

CHUNKS = (6, 6, 4)
QUARTERS = (4, 4, 4, 4)
VMEM = pl.BlockSpec(memory_space=pltpu.VMEM)
SMEM = pl.BlockSpec(memory_space=pltpu.SMEM)
HBM = pl.BlockSpec(memory_space=pltpu.HBM)
ANY = pl.BlockSpec(memory_space=pl.ANY)
PIECES = 4
SCALE = 0.1


def line_ring(n):
    odd = list(range(1, n, 2))
    even = list(range(0, n, 2))
    return [0] + odd + even[:0:-1]


def ring_position(z, n):
    return jnp.where(z == 0, 0, jnp.where(z % 2 == 1, (z + 1) // 2, n - z // 2))


def call(kernel, name, shapes, specs, args, limit=8, scratch=(), flops=0, aliases=None, after=(), out_specs=None):
    args = (*args, *after)
    specs = [*specs, *[ANY] * len(after)]
    count = len(args) - len(after)

    def body(*refs):
        kernel(*refs[:count], *refs[len(args) :])

    return pl.pallas_call(
        body,
        in_specs=specs,
        out_specs=out_specs or [VMEM] * len(shapes),
        out_shape=shapes,
        scratch_shapes=scratch,
        input_output_aliases=aliases or {},
        compiler_params=pltpu.CompilerParams(vmem_limit_bytes=limit << 20),
        cost_estimate=pl.CostEstimate(flops=int(SCALE * flops), bytes_accessed=0, transcendentals=0),
        name=name,
    )(*args)


def times(rows, train_part):
    return lax.dot_general(
        rows, train_part, (((1,), (1,)), ((), ())), preferred_element_type=jnp.float32
    )


def fetch(train, spans, after=(), query=None, precond=None, query_spans=(), rates=()):
    count = train.shape[0]
    tall = count // PIECES
    made = len(query_spans)
    first, total = (query_spans[0][0], sum(width for _, width in query_spans)) if made else (0, 0)

    def kernel(train_ref, *refs):
        copies = []
        if rates:
            *refs, plan, order, rate_sems = refs
            plan_ref, order_ref, *refs = refs
            rate_copies = [
                pltpu.make_async_copy(plan_ref, plan, rate_sems.at[0]),
                pltpu.make_async_copy(order_ref, order, rate_sems.at[1]),
            ]
            for copy in rate_copies:
                copy.start()
        if made:
            query_ref, precond_ref, *refs, held, scale, query_sems = refs
            copies.append(pltpu.make_async_copy(precond_ref.at[:, pl.ds(first, total)], scale, query_sems.at[made]))
            copies += [
                pltpu.make_async_copy(
                    query_ref.at[:, pl.ds(start, width)], held.at[:, pl.ds(start - first, width)], query_sems.at[i]
                )
                for i, (start, width) in enumerate(query_spans)
            ]
        blocks, outs, sems = refs[:made], refs[made : made + len(spans)], refs[-1]
        for copy in copies:
            copy.start()
        train_copies = [
            pltpu.make_async_copy(
                train_ref.at[pl.ds(i * tall, tall), pl.ds(start, width)],
                out.at[pl.ds(i * tall, tall), :],
                sems.at[k, i],
            )
            for k, (out, (start, width)) in enumerate(zip(outs, spans))
            for i in range(PIECES)
        ]
        for copy in train_copies:
            copy.start()
        if made:
            copies[0].wait()
        for i, (start, width) in enumerate(query_spans):
            copies[i + 1].wait()
            at = pl.ds(start - first, width)
            blocks[i][...] = (held[:, at] * scale[:, at]).astype(jnp.bfloat16)
        if rates:
            for copy in rate_copies:
                copy.wait()
            row = refs[made + len(spans)]
            row[...] = jnp.full(row.shape, plan[order[lax.axis_index("ckpt")]], jnp.float32)
        for copy in train_copies:
            copy.wait()

    rows = query.shape[0] if made else 0
    scratch = [pltpu.SemaphoreType.DMA((max(len(spans), 1), PIECES))]
    if made:
        scratch += [
            pltpu.VMEM((rows, total), jnp.float32),
            pltpu.VMEM((1, total), jnp.float32),
            pltpu.SemaphoreType.DMA((made + 1,)),
        ]
    shapes = [jax.ShapeDtypeStruct((rows, width), jnp.bfloat16) for _, width in query_spans]
    shapes += [pltpu.VMEM((count, width), train.dtype) for _, width in spans]
    if rates:
        shapes.append(jax.ShapeDtypeStruct((1, count), jnp.float32))
        scratch += [pltpu.SMEM(array.shape, array.dtype) for array in rates]
        scratch.append(pltpu.SemaphoreType.DMA((2,)))
    return call(
        kernel,
        "fetch" if spans else "condition",
        shapes,
        [ANY] * (1 + len(rates) + (2 if made else 0)),
        (train, *rates, *((query, precond) if made else ())),
        scratch=scratch,
        flops=2 * 512 * sum(width for _, width in spans) * count,
        after=after,
    )


def score(blocks, train, sums=(), picked=(), forward=False, after=()):
    count = len(blocks)
    rows, width = blocks[0].shape
    args = [*blocks, train, *sums, *picked]

    def kernel(*refs):
        given, train_ref, before, outs = refs[:count], refs[count], refs[count + 1 : len(args)], refs[len(args) :]
        stacked = given[0][...] if count == 1 else jnp.concatenate([ref[...] for ref in given], axis=0)
        scores = times(stacked, train_ref[...])
        for i in range(count):
            part = scores[i * rows : (i + 1) * rows]
            if i < len(sums):
                outs[i][...] = before[i][...] + part
            elif picked:
                home, _ = my_pair()

                @pl.when(home)
                def _():
                    outs[i][...] = before[-2][...] + part

                @pl.when(jnp.logical_not(home))
                def _():
                    outs[i][...] = before[-1][...] + part
            else:
                outs[i][...] = part
        if forward:
            outs[count][...] = given[-1][...]

    shapes = [jax.ShapeDtypeStruct((rows, train.shape[0]), jnp.float32)] * count
    if forward:
        shapes.append(jax.ShapeDtypeStruct(blocks[-1].shape, blocks[-1].dtype))
    return call(
        kernel,
        "score",
        shapes,
        [VMEM] * len(args),
        args,
        flops=2 * 256 * width * train.shape[0],
        aliases={count - 1: count} if forward else None,
        after=after,
    )


def sort_out(sums, rate, shards, groups):
    per_group = shards // groups
    rows, columns = sums[0].shape

    def kernel(*refs):
        given, rate_ref, outs = refs[: len(sums)], refs[len(sums)], refs[len(sums) + 1 :]
        my_place = ring_position(lax.axis_index("shard"), shards)
        my_group = lax.axis_index("ckpt") * lax.axis_size("sub") + lax.axis_index("sub")
        for d in range(groups):
            for k in range(per_group):
                chip = (my_group ^ d) * per_group + k
                step = (my_place - ring_position(chip, shards) + shards) % shards
                at = pl.ds((d // 2 * per_group + k) * rows, rows)
                for s, ref in enumerate(given):

                    @pl.when(step == s)
                    def _():
                        outs[1 - d % 2][at, :] = ref[...] * rate_ref[...]

    shape = jax.ShapeDtypeStruct((groups // 2 * per_group * rows, columns), jnp.float32)
    return call(kernel, "sort_out", [shape] * 2, [VMEM] * (len(sums) + 1), (*sums, rate))


def fold(kept, received, tall):
    pieces = kept.shape[0] // tall

    def kernel(kept_ref, received_ref, *outs):
        if pieces == 1:
            outs[0][...] = kept_ref[...] + received_ref[...]
            return
        for i in range(pieces):
            at = pl.ds(i * tall, tall)
            outs[1 - i % 2][pl.ds(i // 2 * tall, tall), :] = kept_ref[at, :] + received_ref[at, :]

    shapes = [jax.ShapeDtypeStruct((max(pieces // 2, 1) * tall, kept.shape[1]), jnp.float32)] * min(pieces, 2)
    return call(kernel, "fold", shapes, [VMEM] * 2, (kept, received))


def my_pair():
    z = lax.axis_index("shard")
    return z // 2 == lax.axis_index("ckpt"), z % 2 == lax.axis_index("sub")


def deal(own, far, after=()):
    def kernel(own_ref, far_ref, first, second):
        home, _ = my_pair()

        @pl.when(home)
        def _():
            first[...] = far_ref[...]
            second[...] = own_ref[...]

        @pl.when(jnp.logical_not(home))
        def _():
            first[...] = own_ref[...]
            second[...] = far_ref[...]

    shape = jax.ShapeDtypeStruct(own.shape, own.dtype)
    return call(kernel, "deal", [shape] * 2, [VMEM] * 2, (own, far), after=after)


def hand_on(array, after):
    def kernel(_, __):
        pass

    shape = jax.ShapeDtypeStruct(array.shape, array.dtype)
    return call(kernel, "hand_on", [shape], [ANY], (array,), after=after, aliases={0: 0}, out_specs=[ANY])[0]


def part_pair(if_home, if_not, other, rate, after=()):
    def kernel(home_ref, not_ref, other_ref, rate_ref, sent, kept):
        home, agree = my_pair()
        for one, ref in ((home, home_ref), (jnp.logical_not(home), not_ref)):

            @pl.when(jnp.logical_and(one, agree))
            def _():
                kept[...] = ref[...] * rate_ref[...]
                sent[...] = other_ref[...] * rate_ref[...]

            @pl.when(jnp.logical_and(one, jnp.logical_not(agree)))
            def _():
                sent[...] = ref[...] * rate_ref[...]
                kept[...] = other_ref[...] * rate_ref[...]

    shape = jax.ShapeDtypeStruct(other.shape, jnp.float32)
    return call(kernel, "part_pair", [shape] * 2, [VMEM] * 4, (if_home, if_not, other, rate), after=after)


def add(*arrays):
    def kernel(*refs):
        total = refs[0][...]
        for ref in refs[1:-1]:
            total = total + ref[...]
        refs[-1][...] = total

    shape = jax.ShapeDtypeStruct(arrays[0].shape, jnp.float32)
    return call(kernel, "add", [shape], [VMEM] * len(arrays), arrays)[0]


def in_pairs(train, query, precond, learn_rates, ckpt_order):
    def swap(array, axis, distance):
        size = lax.axis_size(axis)
        return lax.ppermute(array, axis, [(i, i ^ distance) for i in range(size)])

    unit = query.shape[1] // sum(QUARTERS)
    spans = [(unit * sum(QUARTERS[:j]), unit * c) for j, c in enumerate(QUARTERS)]

    own1, own2 = fetch(train, [], [], query, precond, spans[:2])
    two1 = swap(own1, "shard", 2)
    one1 = swap(own1, "shard", 1)
    two2 = swap(own2, "shard", 2)
    one2 = swap(own2, "shard", 1)
    own3, own4, train1, train2, train3, train4, rate = fetch(
        train, spans, [own2], query, precond, spans[2:], (learn_rates, ckpt_order)
    )
    two3 = swap(own3, "shard", 2)
    two4 = swap(own4, "shard", 2)
    two1 = hand_on(two1, [own4, one1])
    three1 = swap(two1, "shard", 1)
    two2 = hand_on(two2, [two1, one2])
    three2 = swap(two2, "shard", 1)

    sums = score([own1, one1, two1, three1], train1, after=[two2])
    first3, second3 = deal(own3, two3, [sums[0]])
    first3 = swap(first3, "shard", 1)
    sums = score([own2, one2, two2, three2], train2, sums, after=[second3])
    first4, second4 = deal(own4, two4, [sums[0]])
    first4 = swap(first4, "shard", 1)
    own_sums, one_sums, two_sums, three_sums = sums
    second3 = swap(hand_on(second3, [first3, second4]), "shard", 1)
    own_sums, two_sums, first_sums = score(
        [own3, two3, first3], train3, [own_sums, two_sums], (three_sums, one_sums), after=[second4]
    )
    second4 = swap(hand_on(second4, [own_sums]), "shard", 1)
    own_sums, two_sums, first_sums = score([own4, two4, first4], train4, [own_sums, two_sums, first_sums])

    sent, kept = part_pair(two_sums, own_sums, first_sums, rate)
    across = add(kept, swap(sent, "sub", 1))
    from_far = swap(across, "ckpt", 1)
    (second_sums,) = score([second3], train3, picked=(one_sums, three_sums), after=[across])
    (second_sums,) = score([second4], train4, [second_sums])
    sent, kept = part_pair(own_sums, two_sums, second_sums, rate)
    return add(kept, from_far, swap(sent, "sub", 1))


def in_ring(sizes, train_local, query_local, precond, learn_rates, ckpt_order):
    shards, groups = sizes[0], sizes[1] * sizes[2]
    ring = line_ring(shards)
    hops = [(ring[i], ring[(i + 1) % shards]) for i in range(shards)]

    unit = query_local.shape[1] // sum(CHUNKS)
    spans = [(unit * sum(CHUNKS[:j]), unit * c) for j, c in enumerate(CHUNKS)]
    own = fetch(train_local, [], [], query_local, precond, spans[:1])
    *held, rate = fetch(train_local, spans[:1], own, rates=(learn_rates, ckpt_order))
    for span in spans[1:]:
        own += fetch(train_local, [], [held[0], own[-1]], query_local, precond, [span])

    sums = []
    current = own
    for step in range(1, shards):
        current = [lax.ppermute(block, "shard", hops) for block in current]
        forward = step < shards - 1
        total = ()
        for j in range(len(CHUNKS)):
            if j >= len(held):
                held += fetch(train_local, spans[j : j + 1], total[:1])
            blocks = [own[j], current[j]] if step == 1 else [current[j]]
            total = score(blocks, held[j], total, forward=forward)
            if forward:
                *total, current[j] = total
        sums += total
    sent, kept = sort_out(sums, rate, shards, groups)
    tall = kept.shape[0] // (groups // 2)
    for i in range(groups.bit_length() - 1):
        received = lax.ppermute(sent, ("ckpt", "sub"), [(g, g ^ 1 << i) for g in range(groups)])
        *more, kept = fold(kept, received, tall)
        sent = more[0] if more else None
    return kept


def per_device(sizes, train_grads, query_grads, precond, learn_rates, ckpt_order):
    args = [train_grads[0], query_grads[0], precond, learn_rates, ckpt_order]
    args = [pltpu.with_memory_space_constraint(array, pltpu.HBM) for array in args]
    return in_pairs(*args) if sizes == (4, 2, 2) else in_ring(sizes, *args)


def solution(mesh):
    sizes = tuple(mesh.shape[axis] for axis in ("shard", "ckpt", "sub"))

    def run(*args):
        return per_device(sizes, *args)

    return jax.shard_map(
        run,
        mesh=mesh,
        in_specs=(
            P("ckpt", ("parts", "shard"), "sub"),
            P("ckpt", ("parts", "shard"), "sub"),
            P("ckpt", "sub"),
            P(),
            P(),
        ),
        out_specs=P(("ckpt", "sub"), ("parts", "shard")),
        check_vma=False,
    )
```

```python
import jax
import jax.numpy as jnp
from jax import lax
from jax.experimental import pallas as pl
from jax.experimental.pallas import tpu as pltpu
from jax.sharding import PartitionSpec as P

CHUNKS = (6, 6, 4)
QUARTERS = (4, 4, 4, 4)
VMEM = pl.BlockSpec(memory_space=pltpu.VMEM)
SMEM = pl.BlockSpec(memory_space=pltpu.SMEM)
HBM = pl.BlockSpec(memory_space=pltpu.HBM)
ANY = pl.BlockSpec(memory_space=pl.ANY)
PIECES = 4
SCALE = 0.1


def line_ring(n):
    odd = list(range(1, n, 2))
    even = list(range(0, n, 2))
    return [0] + odd + even[:0:-1]


def ring_position(z, n):
    return jnp.where(z == 0, 0, jnp.where(z % 2 == 1, (z + 1) // 2, n - z // 2))


def call(kernel, name, shapes, specs, args, limit=8, scratch=(), flops=0, aliases=None, after=(), out_specs=None):
    args = (*args, *after)
    specs = [*specs, *[ANY] * len(after)]
    count = len(args) - len(after)

    def body(*refs):
        kernel(*refs[:count], *refs[len(args) :])

    return pl.pallas_call(
        body,
        in_specs=specs,
        out_specs=out_specs or [VMEM] * len(shapes),
        out_shape=shapes,
        scratch_shapes=scratch,
        input_output_aliases=aliases or {},
        compiler_params=pltpu.CompilerParams(vmem_limit_bytes=limit << 20),
        cost_estimate=pl.CostEstimate(flops=int(SCALE * flops), bytes_accessed=0, transcendentals=0),
        name=name,
    )(*args)


def times(rows, train_part):
    return lax.dot_general(
        rows, train_part, (((1,), (1,)), ((), ())), preferred_element_type=jnp.float32
    )


def fetch(train, spans, after=(), query=None, precond=None, query_spans=(), rates=()):
    count = train.shape[0]
    tall = count // PIECES
    made = len(query_spans)
    first, total = (query_spans[0][0], sum(width for _, width in query_spans)) if made else (0, 0)

    def kernel(train_ref, *refs):
        copies = []
        if rates:
            *refs, plan, order, rate_sems = refs
            plan_ref, order_ref, *refs = refs
            rate_copies = [
                pltpu.make_async_copy(plan_ref, plan, rate_sems.at[0]),
                pltpu.make_async_copy(order_ref, order, rate_sems.at[1]),
            ]
            for copy in rate_copies:
                copy.start()
        if made:
            query_ref, precond_ref, *refs, held, scale, query_sems = refs
            copies.append(pltpu.make_async_copy(precond_ref.at[:, pl.ds(first, total)], scale, query_sems.at[made]))
            copies += [
                pltpu.make_async_copy(
                    query_ref.at[:, pl.ds(start, width)], held.at[:, pl.ds(start - first, width)], query_sems.at[i]
                )
                for i, (start, width) in enumerate(query_spans)
            ]
        blocks, outs, sems = refs[:made], refs[made : made + len(spans)], refs[-1]
        for copy in copies:
            copy.start()
        train_copies = [
            pltpu.make_async_copy(
                train_ref.at[pl.ds(i * tall, tall), pl.ds(start, width)],
                out.at[pl.ds(i * tall, tall), :],
                sems.at[k, i],
            )
            for k, (out, (start, width)) in enumerate(zip(outs, spans))
            for i in range(PIECES)
        ]
        for copy in train_copies:
            copy.start()
        if made:
            copies[0].wait()
        for i, (start, width) in enumerate(query_spans):
            copies[i + 1].wait()
            at = pl.ds(start - first, width)
            blocks[i][...] = (held[:, at] * scale[:, at]).astype(jnp.bfloat16)
        if rates:
            for copy in rate_copies:
                copy.wait()
            row = refs[made + len(spans)]
            row[...] = jnp.full(row.shape, plan[order[lax.axis_index("ckpt")]], jnp.float32)
        for copy in train_copies:
            copy.wait()

    rows = query.shape[0] if made else 0
    scratch = [pltpu.SemaphoreType.DMA((max(len(spans), 1), PIECES))]
    if made:
        scratch += [
            pltpu.VMEM((rows, total), jnp.float32),
            pltpu.VMEM((1, total), jnp.float32),
            pltpu.SemaphoreType.DMA((made + 1,)),
        ]
    shapes = [jax.ShapeDtypeStruct((rows, width), jnp.bfloat16) for _, width in query_spans]
    shapes += [pltpu.VMEM((count, width), train.dtype) for _, width in spans]
    if rates:
        shapes.append(jax.ShapeDtypeStruct((1, count), jnp.float32))
        scratch += [pltpu.SMEM(array.shape, array.dtype) for array in rates]
        scratch.append(pltpu.SemaphoreType.DMA((2,)))
    return call(
        kernel,
        "fetch" if spans else "condition",
        shapes,
        [ANY] * (1 + len(rates) + (2 if made else 0)),
        (train, *rates, *((query, precond) if made else ())),
        scratch=scratch,
        flops=2 * 512 * sum(width for _, width in spans) * count,
        after=after,
    )


def score(blocks, train, sums=(), picked=(), forward=False, after=()):
    count = len(blocks)
    rows, width = blocks[0].shape
    args = [*blocks, train, *sums, *picked]

    def kernel(*refs):
        given, train_ref, before, outs = refs[:count], refs[count], refs[count + 1 : len(args)], refs[len(args) :]
        stacked = given[0][...] if count == 1 else jnp.concatenate([ref[...] for ref in given], axis=0)
        scores = times(stacked, train_ref[...])
        for i in range(count):
            part = scores[i * rows : (i + 1) * rows]
            if i < len(sums):
                outs[i][...] = before[i][...] + part
            elif picked:
                home, _ = my_pair()

                @pl.when(home)
                def _():
                    outs[i][...] = before[-2][...] + part

                @pl.when(jnp.logical_not(home))
                def _():
                    outs[i][...] = before[-1][...] + part
            else:
                outs[i][...] = part
        if forward:
            outs[count][...] = given[-1][...]

    shapes = [jax.ShapeDtypeStruct((rows, train.shape[0]), jnp.float32)] * count
    if forward:
        shapes.append(jax.ShapeDtypeStruct(blocks[-1].shape, blocks[-1].dtype))
    return call(
        kernel,
        "score",
        shapes,
        [VMEM] * len(args),
        args,
        flops=2 * 256 * width * train.shape[0],
        aliases={count - 1: count} if forward else None,
        after=after,
    )


def sort_out(sums, rate, shards, groups):
    per_group = shards // groups
    rows, columns = sums[0].shape

    def kernel(*refs):
        given, rate_ref, outs = refs[: len(sums)], refs[len(sums)], refs[len(sums) + 1 :]
        my_place = ring_position(lax.axis_index("shard"), shards)
        my_group = lax.axis_index("ckpt") * lax.axis_size("sub") + lax.axis_index("sub")
        for d in range(groups):
            for k in range(per_group):
                chip = (my_group ^ d) * per_group + k
                step = (my_place - ring_position(chip, shards) + shards) % shards
                at = pl.ds((d // 2 * per_group + k) * rows, rows)
                for s, ref in enumerate(given):

                    @pl.when(step == s)
                    def _():
                        outs[1 - d % 2][at, :] = ref[...] * rate_ref[...]

    shape = jax.ShapeDtypeStruct((groups // 2 * per_group * rows, columns), jnp.float32)
    return call(kernel, "sort_out", [shape] * 2, [VMEM] * (len(sums) + 1), (*sums, rate))


def fold(kept, received, tall):
    pieces = kept.shape[0] // tall

    def kernel(kept_ref, received_ref, *outs):
        if pieces == 1:
            outs[0][...] = kept_ref[...] + received_ref[...]
            return
        for i in range(pieces):
            at = pl.ds(i * tall, tall)
            outs[1 - i % 2][pl.ds(i // 2 * tall, tall), :] = kept_ref[at, :] + received_ref[at, :]

    shapes = [jax.ShapeDtypeStruct((max(pieces // 2, 1) * tall, kept.shape[1]), jnp.float32)] * min(pieces, 2)
    return call(kernel, "fold", shapes, [VMEM] * 2, (kept, received))


def my_pair():
    z = lax.axis_index("shard")
    return z // 2 == lax.axis_index("ckpt"), z % 2 == lax.axis_index("sub")


def deal(own, far, after=()):
    def kernel(own_ref, far_ref, first, second):
        home, _ = my_pair()

        @pl.when(home)
        def _():
            first[...] = far_ref[...]
            second[...] = own_ref[...]

        @pl.when(jnp.logical_not(home))
        def _():
            first[...] = own_ref[...]
            second[...] = far_ref[...]

    shape = jax.ShapeDtypeStruct(own.shape, own.dtype)
    return call(kernel, "deal", [shape] * 2, [VMEM] * 2, (own, far), after=after)


def hand_on(array, after):
    def kernel(_, __):
        pass

    shape = jax.ShapeDtypeStruct(array.shape, array.dtype)
    return call(kernel, "hand_on", [shape], [ANY], (array,), after=after, aliases={0: 0}, out_specs=[ANY])[0]


def score_and_part(blocks, train, sums, rate, near=(), after=()):
    count = len(blocks)
    rows = blocks[0].shape[0]
    args = [*blocks, train, *sums, rate, *near]

    def kernel(*refs):
        given, train_ref, before = refs[:count], refs[count], refs[count + 1 : 2 * count + 1]
        rate_ref, pair, outs = refs[2 * count + 1], refs[2 * count + 2 : len(args)], refs[len(args) :]
        *totals_out, sent, kept = outs
        stacked = given[0][...] if count == 1 else jnp.concatenate([ref[...] for ref in given], axis=0)
        scores = times(stacked, train_ref[...])
        for i, out in enumerate(totals_out):
            out[...] = before[i][...] + scores[i * rows : (i + 1) * rows]
        last = (before[-1][...] + scores[(count - 1) * rows :]) * rate_ref[...]
        home, agree = my_pair()
        at_home, elsewhere = pair or (totals_out[1], totals_out[0])
        for one, ref in ((home, at_home), (jnp.logical_not(home), elsewhere)):

            @pl.when(jnp.logical_and(one, agree))
            def _():
                kept[...] = ref[...] * rate_ref[...]
                sent[...] = last

            @pl.when(jnp.logical_and(one, jnp.logical_not(agree)))
            def _():
                sent[...] = ref[...] * rate_ref[...]
                kept[...] = last

    shape = jax.ShapeDtypeStruct((rows, train.shape[0]), jnp.float32)
    flops = 2 * 256 * train.shape[1] * train.shape[0]
    shapes = [shape] * (2 + (0 if near else count - 1))
    return call(kernel, "score_and_part", shapes, [VMEM] * len(args), args, flops=flops, after=after)


def add(*arrays):
    def kernel(*refs):
        total = refs[0][...]
        for ref in refs[1:-1]:
            total = total + ref[...]
        refs[-1][...] = total

    shape = jax.ShapeDtypeStruct(arrays[0].shape, jnp.float32)
    return call(kernel, "add", [shape], [VMEM] * len(arrays), arrays)[0]


def in_pairs(train, query, precond, learn_rates, ckpt_order):
    def swap(array, axis, distance):
        size = lax.axis_size(axis)
        return lax.ppermute(array, axis, [(i, i ^ distance) for i in range(size)])

    unit = query.shape[1] // sum(QUARTERS)
    spans = [(unit * sum(QUARTERS[:j]), unit * c) for j, c in enumerate(QUARTERS)]

    own1, own2 = fetch(train, [], [], query, precond, spans[:2])
    two1 = swap(own1, "shard", 2)
    one1 = swap(own1, "shard", 1)
    two2 = swap(own2, "shard", 2)
    one2 = swap(own2, "shard", 1)
    own3, own4, train1, train2, train3, train4, rate = fetch(
        train, spans, [own2], query, precond, spans[2:], (learn_rates, ckpt_order)
    )
    two3 = swap(own3, "shard", 2)
    two4 = swap(own4, "shard", 2)
    two1 = hand_on(two1, [own4, one1])
    three1 = swap(two1, "shard", 1)
    two2 = hand_on(two2, [two1, one2])
    three2 = swap(two2, "shard", 1)

    sums = score([own1, one1, two1, three1], train1, after=[two2])
    first3, second3 = deal(own3, two3, [sums[0]])
    first3 = swap(first3, "shard", 1)
    sums = score([own2, one2, two2, three2], train2, sums, after=[second3])
    first4, second4 = deal(own4, two4, [sums[0]])
    first4 = swap(first4, "shard", 1)
    own_sums, one_sums, two_sums, three_sums = sums
    second3 = swap(hand_on(second3, [first3, second4]), "shard", 1)
    own_sums, two_sums, first_sums = score(
        [own3, two3, first3], train3, [own_sums, two_sums], (three_sums, one_sums), after=[second4]
    )
    second4 = swap(hand_on(second4, [own_sums]), "shard", 1)
    own_sums, two_sums, sent, kept = score_and_part(
        [own4, two4, first4], train4, [own_sums, two_sums, first_sums], rate
    )
    across = add(kept, swap(sent, "sub", 1))
    from_far = swap(across, "ckpt", 1)
    (second_sums,) = score([second3], train3, picked=(one_sums, three_sums), after=[across])
    sent, kept = score_and_part([second4], train4, [second_sums], rate, (own_sums, two_sums))
    return add(kept, from_far, swap(sent, "sub", 1))


def in_ring(sizes, train_local, query_local, precond, learn_rates, ckpt_order):
    shards, groups = sizes[0], sizes[1] * sizes[2]
    ring = line_ring(shards)
    hops = [(ring[i], ring[(i + 1) % shards]) for i in range(shards)]

    unit = query_local.shape[1] // sum(CHUNKS)
    spans = [(unit * sum(CHUNKS[:j]), unit * c) for j, c in enumerate(CHUNKS)]
    own = fetch(train_local, [], [], query_local, precond, spans[:1])
    *held, rate = fetch(train_local, spans[:1], own, rates=(learn_rates, ckpt_order))
    for span in spans[1:]:
        own += fetch(train_local, [], [held[0], own[-1]], query_local, precond, [span])

    sums = []
    current = own
    for step in range(1, shards):
        current = [lax.ppermute(block, "shard", hops) for block in current]
        forward = step < shards - 1
        total = ()
        for j in range(len(CHUNKS)):
            if j >= len(held):
                held += fetch(train_local, spans[j : j + 1], total[:1])
            blocks = [own[j], current[j]] if step == 1 else [current[j]]
            total = score(blocks, held[j], total, forward=forward)
            if forward:
                *total, current[j] = total
        sums += total
    sent, kept = sort_out(sums, rate, shards, groups)
    tall = kept.shape[0] // (groups // 2)
    for i in range(groups.bit_length() - 1):
        received = lax.ppermute(sent, ("ckpt", "sub"), [(g, g ^ 1 << i) for g in range(groups)])
        *more, kept = fold(kept, received, tall)
        sent = more[0] if more else None
    return kept


def per_device(sizes, train_grads, query_grads, precond, learn_rates, ckpt_order):
    args = [train_grads[0], query_grads[0], precond, learn_rates, ckpt_order]
    args = [pltpu.with_memory_space_constraint(array, pltpu.HBM) for array in args]
    return in_pairs(*args) if sizes == (4, 2, 2) else in_ring(sizes, *args)


def solution(mesh):
    sizes = tuple(mesh.shape[axis] for axis in ("shard", "ckpt", "sub"))

    def run(*args):
        return per_device(sizes, *args)

    return jax.shard_map(
        run,
        mesh=mesh,
        in_specs=(
            P("ckpt", ("parts", "shard"), "sub"),
            P("ckpt", ("parts", "shard"), "sub"),
            P("ckpt", "sub"),
            P(),
            P(),
        ),
        out_specs=P(("ckpt", "sub"), ("parts", "shard")),
        check_vma=False,
    )
```

```python
import jax
import jax.numpy as jnp
from jax import lax
from jax.experimental import pallas as pl
from jax.experimental.pallas import tpu as pltpu
from jax.sharding import PartitionSpec as P

CHUNKS = (6, 6, 4)
QUARTERS = (17, 16, 16, 15)
VMEM = pl.BlockSpec(memory_space=pltpu.VMEM)
SMEM = pl.BlockSpec(memory_space=pltpu.SMEM)
HBM = pl.BlockSpec(memory_space=pltpu.HBM)
ANY = pl.BlockSpec(memory_space=pl.ANY)
PIECES = 4
SCALE = 0.1


def line_ring(n):
    odd = list(range(1, n, 2))
    even = list(range(0, n, 2))
    return [0] + odd + even[:0:-1]


def ring_position(z, n):
    return jnp.where(z == 0, 0, jnp.where(z % 2 == 1, (z + 1) // 2, n - z // 2))


def call(kernel, name, shapes, specs, args, limit=8, scratch=(), flops=0, aliases=None, after=(), out_specs=None):
    args = (*args, *after)
    specs = [*specs, *[ANY] * len(after)]
    count = len(args) - len(after)

    def body(*refs):
        kernel(*refs[:count], *refs[len(args) :])

    return pl.pallas_call(
        body,
        in_specs=specs,
        out_specs=out_specs or [VMEM] * len(shapes),
        out_shape=shapes,
        scratch_shapes=scratch,
        input_output_aliases=aliases or {},
        compiler_params=pltpu.CompilerParams(vmem_limit_bytes=limit << 20),
        cost_estimate=pl.CostEstimate(flops=int(SCALE * flops), bytes_accessed=0, transcendentals=0),
        name=name,
    )(*args)


def times(rows, train_part):
    return lax.dot_general(
        rows, train_part, (((1,), (1,)), ((), ())), preferred_element_type=jnp.float32
    )


def fetch(train, spans, after=(), query=None, precond=None, query_spans=(), rates=()):
    count = train.shape[0]
    tall = count // PIECES
    made = len(query_spans)
    first, total = (query_spans[0][0], sum(width for _, width in query_spans)) if made else (0, 0)

    def kernel(train_ref, *refs):
        copies = []
        if rates:
            *refs, plan, order, rate_sems = refs
            plan_ref, order_ref, *refs = refs
            rate_copies = [
                pltpu.make_async_copy(plan_ref, plan, rate_sems.at[0]),
                pltpu.make_async_copy(order_ref, order, rate_sems.at[1]),
            ]
            for copy in rate_copies:
                copy.start()
        if made:
            query_ref, precond_ref, *refs, held, scale, query_sems = refs
            copies.append(pltpu.make_async_copy(precond_ref.at[:, pl.ds(first, total)], scale, query_sems.at[made]))
            copies += [
                pltpu.make_async_copy(
                    query_ref.at[:, pl.ds(start, width)], held.at[:, pl.ds(start - first, width)], query_sems.at[i]
                )
                for i, (start, width) in enumerate(query_spans)
            ]
        blocks, outs, sems = refs[:made], refs[made : made + len(spans)], refs[-1]
        for copy in copies:
            copy.start()
        train_copies = [
            pltpu.make_async_copy(
                train_ref.at[pl.ds(i * tall, tall), pl.ds(start, width)],
                out.at[pl.ds(i * tall, tall), :],
                sems.at[k, i],
            )
            for k, (out, (start, width)) in enumerate(zip(outs, spans))
            for i in range(PIECES)
        ]
        for copy in train_copies:
            copy.start()
        if made:
            copies[0].wait()
        for i, (start, width) in enumerate(query_spans):
            copies[i + 1].wait()
            at = pl.ds(start - first, width)
            blocks[i][...] = (held[:, at] * scale[:, at]).astype(jnp.bfloat16)
        if rates:
            for copy in rate_copies:
                copy.wait()
            row = refs[made + len(spans)]
            row[...] = jnp.full(row.shape, plan[order[lax.axis_index("ckpt")]], jnp.float32)
        for copy in train_copies:
            copy.wait()

    rows = query.shape[0] if made else 0
    scratch = [pltpu.SemaphoreType.DMA((max(len(spans), 1), PIECES))]
    if made:
        scratch += [
            pltpu.VMEM((rows, total), jnp.float32),
            pltpu.VMEM((1, total), jnp.float32),
            pltpu.SemaphoreType.DMA((made + 1,)),
        ]
    shapes = [jax.ShapeDtypeStruct((rows, width), jnp.bfloat16) for _, width in query_spans]
    shapes += [pltpu.VMEM((count, width), train.dtype) for _, width in spans]
    if rates:
        shapes.append(jax.ShapeDtypeStruct((1, count), jnp.float32))
        scratch += [pltpu.SMEM(array.shape, array.dtype) for array in rates]
        scratch.append(pltpu.SemaphoreType.DMA((2,)))
    return call(
        kernel,
        "fetch" if spans else "condition",
        shapes,
        [ANY] * (1 + len(rates) + (2 if made else 0)),
        (train, *rates, *((query, precond) if made else ())),
        scratch=scratch,
        flops=2 * 512 * sum(width for _, width in spans) * count,
        after=after,
    )


def score(blocks, train, sums=(), picked=(), forward=False, after=()):
    count = len(blocks)
    rows, width = blocks[0].shape
    args = [*blocks, train, *sums, *picked]

    def kernel(*refs):
        given, train_ref, before, outs = refs[:count], refs[count], refs[count + 1 : len(args)], refs[len(args) :]
        stacked = given[0][...] if count == 1 else jnp.concatenate([ref[...] for ref in given], axis=0)
        scores = times(stacked, train_ref[...])
        for i in range(count):
            part = scores[i * rows : (i + 1) * rows]
            if i < len(sums):
                outs[i][...] = before[i][...] + part
            elif picked:
                home, _ = my_pair()

                @pl.when(home)
                def _():
                    outs[i][...] = before[-2][...] + part

                @pl.when(jnp.logical_not(home))
                def _():
                    outs[i][...] = before[-1][...] + part
            else:
                outs[i][...] = part
        if forward:
            outs[count][...] = given[-1][...]

    shapes = [jax.ShapeDtypeStruct((rows, train.shape[0]), jnp.float32)] * count
    if forward:
        shapes.append(jax.ShapeDtypeStruct(blocks[-1].shape, blocks[-1].dtype))
    return call(
        kernel,
        "score",
        shapes,
        [VMEM] * len(args),
        args,
        flops=2 * 256 * width * train.shape[0],
        aliases={count - 1: count} if forward else None,
        after=after,
    )


def sort_out(sums, rate, shards, groups):
    per_group = shards // groups
    rows, columns = sums[0].shape

    def kernel(*refs):
        given, rate_ref, outs = refs[: len(sums)], refs[len(sums)], refs[len(sums) + 1 :]
        my_place = ring_position(lax.axis_index("shard"), shards)
        my_group = lax.axis_index("ckpt") * lax.axis_size("sub") + lax.axis_index("sub")
        for d in range(groups):
            for k in range(per_group):
                chip = (my_group ^ d) * per_group + k
                step = (my_place - ring_position(chip, shards) + shards) % shards
                at = pl.ds((d // 2 * per_group + k) * rows, rows)
                for s, ref in enumerate(given):

                    @pl.when(step == s)
                    def _():
                        outs[1 - d % 2][at, :] = ref[...] * rate_ref[...]

    shape = jax.ShapeDtypeStruct((groups // 2 * per_group * rows, columns), jnp.float32)
    return call(kernel, "sort_out", [shape] * 2, [VMEM] * (len(sums) + 1), (*sums, rate))


def fold(kept, received, tall):
    pieces = kept.shape[0] // tall

    def kernel(kept_ref, received_ref, *outs):
        if pieces == 1:
            outs[0][...] = kept_ref[...] + received_ref[...]
            return
        for i in range(pieces):
            at = pl.ds(i * tall, tall)
            outs[1 - i % 2][pl.ds(i // 2 * tall, tall), :] = kept_ref[at, :] + received_ref[at, :]

    shapes = [jax.ShapeDtypeStruct((max(pieces // 2, 1) * tall, kept.shape[1]), jnp.float32)] * min(pieces, 2)
    return call(kernel, "fold", shapes, [VMEM] * 2, (kept, received))


def my_pair():
    z = lax.axis_index("shard")
    return z // 2 == lax.axis_index("ckpt"), z % 2 == lax.axis_index("sub")


def deal(own, far, after=()):
    def kernel(own_ref, far_ref, first, second):
        home, _ = my_pair()

        @pl.when(home)
        def _():
            first[...] = far_ref[...]
            second[...] = own_ref[...]

        @pl.when(jnp.logical_not(home))
        def _():
            first[...] = own_ref[...]
            second[...] = far_ref[...]

    shape = jax.ShapeDtypeStruct(own.shape, own.dtype)
    return call(kernel, "deal", [shape] * 2, [VMEM] * 2, (own, far), after=after)


def hand_on(array, after):
    def kernel(_, __):
        pass

    shape = jax.ShapeDtypeStruct(array.shape, array.dtype)
    return call(kernel, "hand_on", [shape], [ANY], (array,), after=after, aliases={0: 0}, out_specs=[ANY])[0]


def score_and_part(blocks, train, sums, rate, near=(), after=()):
    count = len(blocks)
    rows = blocks[0].shape[0]
    args = [*blocks, train, *sums, rate, *near]

    def kernel(*refs):
        given, train_ref, before = refs[:count], refs[count], refs[count + 1 : 2 * count + 1]
        rate_ref, pair, outs = refs[2 * count + 1], refs[2 * count + 2 : len(args)], refs[len(args) :]
        *totals_out, sent, kept = outs
        stacked = given[0][...] if count == 1 else jnp.concatenate([ref[...] for ref in given], axis=0)
        scores = times(stacked, train_ref[...])
        for i, out in enumerate(totals_out):
            out[...] = before[i][...] + scores[i * rows : (i + 1) * rows]
        last = (before[-1][...] + scores[(count - 1) * rows :]) * rate_ref[...]
        home, agree = my_pair()
        at_home, elsewhere = pair or (totals_out[1], totals_out[0])
        for one, ref in ((home, at_home), (jnp.logical_not(home), elsewhere)):

            @pl.when(jnp.logical_and(one, agree))
            def _():
                kept[...] = ref[...] * rate_ref[...]
                sent[...] = last

            @pl.when(jnp.logical_and(one, jnp.logical_not(agree)))
            def _():
                sent[...] = ref[...] * rate_ref[...]
                kept[...] = last

    shape = jax.ShapeDtypeStruct((rows, train.shape[0]), jnp.float32)
    flops = 2 * 256 * train.shape[1] * train.shape[0]
    shapes = [shape] * (2 + (0 if near else count - 1))
    return call(kernel, "score_and_part", shapes, [VMEM] * len(args), args, flops=flops, after=after)


def add(*arrays):
    def kernel(*refs):
        total = refs[0][...]
        for ref in refs[1:-1]:
            total = total + ref[...]
        refs[-1][...] = total

    shape = jax.ShapeDtypeStruct(arrays[0].shape, jnp.float32)
    return call(kernel, "add", [shape], [VMEM] * len(arrays), arrays)[0]


def in_pairs(train, query, precond, learn_rates, ckpt_order):
    def swap(array, axis, distance):
        size = lax.axis_size(axis)
        return lax.ppermute(array, axis, [(i, i ^ distance) for i in range(size)])

    unit = query.shape[1] // sum(QUARTERS)
    spans = [(unit * sum(QUARTERS[:j]), unit * c) for j, c in enumerate(QUARTERS)]

    own1, own2 = fetch(train, [], [], query, precond, spans[:2])
    two1 = swap(own1, "shard", 2)
    one1 = swap(own1, "shard", 1)
    two2 = swap(own2, "shard", 2)
    one2 = swap(own2, "shard", 1)
    own3, own4, train1, train2, train3, train4, rate = fetch(
        train, spans, [own2], query, precond, spans[2:], (learn_rates, ckpt_order)
    )
    two3 = swap(own3, "shard", 2)
    two4 = swap(own4, "shard", 2)
    two1 = hand_on(two1, [own4, one1])
    three1 = swap(two1, "shard", 1)
    two2 = hand_on(two2, [two1, one2])
    three2 = swap(two2, "shard", 1)

    sums = score([own1, one1, two1, three1], train1, after=[two2])
    first3, second3 = deal(own3, two3, [sums[0]])
    first3 = swap(first3, "shard", 1)
    sums = score([own2, one2, two2, three2], train2, sums, after=[second3])
    first4, second4 = deal(own4, two4, [sums[0]])
    first4 = swap(first4, "shard", 1)
    own_sums, one_sums, two_sums, three_sums = sums
    second3 = swap(hand_on(second3, [first3, second4]), "shard", 1)
    own_sums, two_sums, first_sums = score(
        [own3, two3, first3], train3, [own_sums, two_sums], (three_sums, one_sums), after=[second4]
    )
    second4 = swap(hand_on(second4, [own_sums]), "shard", 1)
    own_sums, two_sums, sent, kept = score_and_part(
        [own4, two4, first4], train4, [own_sums, two_sums, first_sums], rate
    )
    across = add(kept, swap(sent, "sub", 1))
    from_far = swap(across, "ckpt", 1)
    (second_sums,) = score([second3], train3, picked=(one_sums, three_sums), after=[sent])
    sent, kept = score_and_part([second4], train4, [second_sums], rate, (own_sums, two_sums))
    return add(kept, from_far, swap(sent, "sub", 1))


def in_ring(sizes, train_local, query_local, precond, learn_rates, ckpt_order):
    shards, groups = sizes[0], sizes[1] * sizes[2]
    ring = line_ring(shards)
    hops = [(ring[i], ring[(i + 1) % shards]) for i in range(shards)]

    unit = query_local.shape[1] // sum(CHUNKS)
    spans = [(unit * sum(CHUNKS[:j]), unit * c) for j, c in enumerate(CHUNKS)]
    own = fetch(train_local, [], [], query_local, precond, spans[:1])
    *held, rate = fetch(train_local, spans[:1], own, rates=(learn_rates, ckpt_order))
    for span in spans[1:]:
        own += fetch(train_local, [], [held[0], own[-1]], query_local, precond, [span])

    sums = []
    current = own
    for step in range(1, shards):
        current = [lax.ppermute(block, "shard", hops) for block in current]
        forward = step < shards - 1
        total = ()
        for j in range(len(CHUNKS)):
            if j >= len(held):
                held += fetch(train_local, spans[j : j + 1], total[:1])
            blocks = [own[j], current[j]] if step == 1 else [current[j]]
            total = score(blocks, held[j], total, forward=forward)
            if forward:
                *total, current[j] = total
        sums += total
    sent, kept = sort_out(sums, rate, shards, groups)
    tall = kept.shape[0] // (groups // 2)
    for i in range(groups.bit_length() - 1):
        received = lax.ppermute(sent, ("ckpt", "sub"), [(g, g ^ 1 << i) for g in range(groups)])
        *more, kept = fold(kept, received, tall)
        sent = more[0] if more else None
    return kept


def per_device(sizes, train_grads, query_grads, precond, learn_rates, ckpt_order):
    args = [train_grads[0], query_grads[0], precond, learn_rates, ckpt_order]
    args = [pltpu.with_memory_space_constraint(array, pltpu.HBM) for array in args]
    return in_pairs(*args) if sizes == (4, 2, 2) else in_ring(sizes, *args)


def solution(mesh):
    sizes = tuple(mesh.shape[axis] for axis in ("shard", "ckpt", "sub"))

    def run(*args):
        return per_device(sizes, *args)

    return jax.shard_map(
        run,
        mesh=mesh,
        in_specs=(
            P("ckpt", ("parts", "shard"), "sub"),
            P("ckpt", ("parts", "shard"), "sub"),
            P("ckpt", "sub"),
            P(),
            P(),
        ),
        out_specs=P(("ckpt", "sub"), ("parts", "shard")),
        check_vma=False,
    )
```
